1024 devices in a mesh: expert: 64 (over z, x), tensor: 16 (over y, core).
Axes of the slice: x: 4, y: 8, z: 16, core: 2. Of those that a mesh axis runs over, the one named last changes fastest.
Arguments:
- out_grad: bfloat16 [7168, 3584], P('expert', 'tensor'), may hold values from -6 to 6
- dense_pre: bfloat16 [7168, 2, 2432], P('expert', None, 'tensor'), may hold values from -5 to 5
- dense_in: bfloat16 [2, 2432, 3584], P(None, 'tensor'), may hold values from -0.125 to 0.125
- dense_out: bfloat16 [2432, 3584], P('tensor'), may hold values from -0.09375 to 0.09375
- routes: int32 [7168, 2], P('expert'), may hold values from 0 to 63, all different within a row; in each aligned block of 112 rows (0 to 111, 112 to 223, ...) at most 4 rows name the same one
- combine: float32 [7168, 2], P('expert'), may hold values from 0.1 to 1
- expert_pre: bfloat16 [64, 256, 2, 2432], P('expert', None, None, 'tensor'), may hold values from -5 to 5
- expert_in: bfloat16 [64, 2, 2432, 3584], P('expert', None, 'tensor'), may hold values from -0.125 to 0.125
- expert_out: bfloat16 [64, 2432, 3584], P('expert', 'tensor'), may hold values from -0.09375 to 0.09375
Outputs:
- in_grad: bfloat16 [7168, 3584], P('expert', 'tensor')
The draws below stay inside these ranges and needn't reach their ends.
Inputs may be any that keep to these rules, and one draw needn't show every extreme that they name: `routes`: the two experts of a token differ. Among the tokens of one group of 112, no expert is named more than 4 times, a bound that some block reaches.
All inputs are finite; a program needn't handle non-finite values.
Results may differ from the reference program's by a relative error of at most 0.0049.
Values may be sent and summed in bfloat16 or wider, within the bound.
A program may use at most 64 MiB of HBM per device.

```python
import math
import jax
import jax.numpy as jnp
import numpy as np
from jax import lax

D = 3584
FF = 2432
TOK_GRP = 112
EXPERTS = 64
CAP = 4
SLOTS = 256
TOKENS = 7168
N_EXPERT = 64


def level_of(own_key, shape, pieces, low, largest):
    def one(dim, parts):
        heights = jax.random.uniform(jax.random.fold_in(jax.random.fold_in(own_key, 6), dim), (parts,), jnp.float32, low / len(pieces), largest / len(pieces))
        return jnp.repeat(jnp.exp(heights), shape[dim] // parts).reshape((-1,) + (1,) * (len(shape) - dim - 1))

    level = one(*pieces[0])
    for cut in pieces[1:]:
        level = level * one(*cut)
    return level


def deal_out(rng, own, number, rows, number_of, top, most, slope):
    ranking = jax.random.permutation(rng, number_of)
    packed, ordinary = shares(number_of, rows * top, most, slope, True), shares(number_of, rows * top, most, slope, False)
    places = jnp.arange(number_of)

    def named(tallies, offset_by):
        used = int((tallies > 0).sum())
        fixed = max(1, used // 4)
        shifted = fixed + (places - fixed + offset_by * (used - fixed)) % max(1, number_of - fixed)
        return jnp.zeros((number_of,), jnp.int32).at[ranking[jnp.where(places < fixed, places, shifted)]].set(jnp.asarray(tallies, jnp.int32))

    tallies = jnp.where(number % 4 == 0, named(packed, number // 4), named(ordinary, number - number // 4 - 1))
    mixed = jax.random.permutation(jax.random.fold_in(own, 3), number_of)
    source_of, receiver = mixed[0:number_of // 2 * 2:2], mixed[1:number_of // 2 * 2:2]
    room = jnp.minimum(tallies[source_of] - 1, most - tallies[receiver]) // 2
    room = jnp.where((source_of == ranking[0]) | (receiver == ranking[0]) | (tallies[receiver] == 0), 0, jnp.maximum(room, 0))
    shifted = jax.random.randint(jax.random.fold_in(own, 4), (number_of // 2,), 0, 1 << 20) % (room + 1)
    tallies = tallies.at[source_of].add(-shifted).at[receiver].add(shifted)
    labels = jnp.searchsorted(jnp.cumsum(tallies), jnp.arange(rows * top), side="right").astype(jnp.int32)
    table = labels.reshape(top, rows).T
    table = table[jax.random.permutation(jax.random.fold_in(own, 1), rows)]
    offset_by = jax.random.randint(jax.random.fold_in(own, 2), (rows, 1), 0, top)
    return jnp.take_along_axis(table, (jnp.arange(top)[None, :] + offset_by) % top, axis=1)


def shares(amount, total, limit, slope, full):
    weights = [(1 << 20) // math.isqrt(rank ** slope) + 1 for rank in range(1, amount + 1)]
    largest = limit if full else min(limit, max(-(-total // amount), total * weights[0] // sum(weights)))
    least = 1 if total - largest >= amount - 1 else 0
    counts, surplus = [largest] + [least] * (amount - 1), total - largest - least * (amount - 1)
    while surplus > 0:
        movable = [i for i in range(1, amount) if counts[i] < largest] or [i for i in range(1, amount) if counts[i] < limit]
        mass, left = sum([weights[i] for i in movable]), surplus
        for i in movable:
            addition = min(limit - counts[i], max(1, left * weights[i] // mass), surplus)
            counts[i] = counts[i] + addition
            surplus = surplus - addition
    return np.array(counts)


def normal_values(rng, shape, spread, most, split=(), held_as=jnp.bfloat16):
    entries = spread * jax.random.normal(rng, shape, jnp.float32)
    if split:
        entries = entries * level_of(rng, shape, split, -0.22, 0.18)
    return jnp.clip(entries, -most, most).astype(held_as)


def setup_inputs(seed: int = 0) -> dict:
    keys = jax.random.split(jax.random.key(seed), 10)
    out_grad = normal_values(keys[0], (TOKENS, D), 1.0, 6.0, ((0, 64), (1, 16)))
    dense_pre = normal_values(keys[1], (TOKENS, 2, FF), 1.0, 5.0, ((0, 64), (2, 16)))
    dense_in = normal_values(keys[2], (2, FF, D), FF ** -0.5, 0.125, ((1, 16),))
    dense_out = normal_values(keys[3], (FF, D), D ** -0.5, 0.09375, ((0, 16),))
    routes_keys = jax.random.split(jax.random.fold_in(keys[4], 1), TOKENS // TOK_GRP)
    routes_turns = jax.random.permutation(jax.random.fold_in(keys[4], 3), TOKENS // TOK_GRP)
    routes = jax.vmap(lambda own, number: deal_out(jax.random.fold_in(keys[4], 2), own, number, TOK_GRP, EXPERTS, 2, CAP, 2))(routes_keys, routes_turns).reshape((TOKENS, 2))
    combine = jnp.clip(0.1 + 0.9 * jax.random.uniform(keys[5], (TOKENS, 2), jnp.float32) ** level_of(keys[5], (TOKENS, 2), ((0, 64),), -0.2, 0.2), 0.1, 1.0)
    expert_pre = normal_values(keys[6], (EXPERTS, SLOTS, 2, FF), 1.0, 5.0, ((0, 64), (3, 16)))
    expert_in = normal_values(keys[7], (EXPERTS, 2, FF, D), FF ** -0.5, 0.125, ((0, 64), (2, 16)))
    expert_out = normal_values(keys[8], (EXPERTS, FF, D), D ** -0.5, 0.09375, ((0, 64), (1, 16)))
    return dict(out_grad=out_grad, dense_pre=dense_pre, dense_in=dense_in, dense_out=dense_out, routes=routes, combine=combine, expert_pre=expert_pre, expert_in=expert_in, expert_out=expert_out)


def swiglu_grads(hidden, saved):
    gate_value = saved[:, 0, :].astype(jnp.float32)
    upper_value = saved[:, 1, :].astype(jnp.float32)
    sigmoid_gate = jax.nn.sigmoid(gate_value)
    gate_grad = (hidden * upper_value * sigmoid_gate * (1.0 + gate_value * (1.0 - sigmoid_gate))).astype(jnp.bfloat16)
    upper_grad = (hidden * gate_value * sigmoid_gate).astype(jnp.bfloat16)
    return gate_grad, upper_grad


def down_back(row_block, w_out):
    return lax.dot_general(row_block, w_out, (((1,), (1,)), ((), ())), preferred_element_type=jnp.float32)


def reference(out_grad, dense_pre, dense_in, dense_out, routes, combine, expert_pre, expert_in, expert_out):
    groups = N_EXPERT
    flat_routes = routes.reshape(groups, TOK_GRP * 2).astype(jnp.int32)
    onehot = (flat_routes[:, :, None] == jnp.arange(EXPERTS, dtype=jnp.int32)[None, None, :]).astype(jnp.int32)
    before = jnp.cumsum(onehot, axis=1) - onehot
    slot_index = jnp.sum(before * onehot, axis=2).astype(jnp.int32)
    group_index = jnp.arange(groups, dtype=jnp.int32)[:, None]
    target = (flat_routes * SLOTS + group_index * CAP + slot_index).reshape(-1).astype(jnp.int32)
    expert_rows = jnp.zeros((EXPERTS * SLOTS, D), jnp.bfloat16).at[target].set(jnp.repeat(out_grad, 2, axis=0))
    expert_rows = expert_rows.reshape(EXPERTS, SLOTS, D)
    dense_hidden = down_back(out_grad, dense_out)
    dense_gate, dense_upper = swiglu_grads(dense_hidden, dense_pre)
    dense_term = jnp.dot(dense_gate, dense_in[0], preferred_element_type=jnp.float32)
    dense_term = dense_term + jnp.dot(dense_upper, dense_in[1], preferred_element_type=jnp.float32)

    def one_expert(operands):
        row_block, saved, w_in, w_out = operands
        hidden = down_back(row_block, w_out)
        gate_grad, upper_grad = swiglu_grads(hidden, saved)
        result = jnp.dot(gate_grad, w_in[0], preferred_element_type=jnp.float32)
        return result + jnp.dot(upper_grad, w_in[1], preferred_element_type=jnp.float32)

    expert_back = lax.map(one_expert, (expert_rows, expert_pre, expert_in, expert_out))
    picked = expert_back.reshape(EXPERTS * SLOTS, D)[target].reshape(TOKENS, 2, D)
    total = dense_term + combine[:, 0:1] * picked[:, 0] + combine[:, 1:2] * picked[:, 1]
    return total.astype(jnp.bfloat16)
```

```python
import functools

import jax
import jax.numpy as jnp
from jax import lax
from jax.experimental import pallas as pl
from jax.experimental.pallas import tpu as pltpu
from jax.sharding import PartitionSpec as P

BF16 = jnp.bfloat16
F32 = jnp.float32
MESH = pl.DeviceIdType.MESH
TN = (((0,), (0,)), ((), ()))
NT = (((1,), (1,)), ((), ()))


def dot(a, b, dims=(((1,), (0,)), ((), ()))):
    return lax.dot_general(a, b, dims, preferred_element_type=F32)


def iota(shape, dim):
    return lax.broadcasted_iota(jnp.int32, shape, dim)


def flag(mask):
    return jnp.where(mask, 1.0, 0.0).astype(BF16)


def kernel(
    sizes,
    og_hbm,
    rt_hbm,
    cb_hbm,
    pre_d_hbm,
    pre_e_hbm,
    out_d_hbm,
    in_d_hbm,
    out_e_hbm,
    in_e_hbm,
    result,
    og,
    rt,
    cb,
    pre_d,
    pre_e,
    w_out,
    w_in,
    w_in_t,
    small,
    picks,
    sent,
    arrived,
    returning,
    returned,
    xt,
    own_part,
    pair_out,
    pair_in,
    ring_out,
    ring_in,
    dense_sum,
    load_sem,
    a2a_send,
    a2a_recv,
    back_send,
    back_recv,
    ag_send,
    ag_ring,
    ag_pair,
    rs_send,
    rs_ring,
    rs_pair,
):
    ne, ny, tok, feat, units, cap, lanes = sizes
    nt = 2 * ny
    far = ny // 2
    half = feat // 2
    rows8 = 2 * cap
    per = ne // 2
    e = lax.axis_index("expert")
    t = lax.axis_index("tensor")
    y = lax.div(t, 2)
    c = lax.rem(t, 2)
    right = lax.rem(y + 1, ny) * 2 + c
    left = lax.rem(y + ny - 1, ny) * 2 + c
    sibling = y * 2 + (1 - c)

    def ring_pos(offset):
        return lax.rem(y + (offset + 2 * ny), ny)

    loads = [
        (rt_hbm, rt),
        (og_hbm, og),
        (cb_hbm, cb),
        (out_d_hbm, w_out.at[0]),
        (in_d_hbm, w_in.at[0]),
        (pre_d_hbm, pre_d),
        (out_e_hbm, w_out.at[1]),
        (in_e_hbm, w_in.at[1]),
        (pre_e_hbm, pre_e),
    ]
    loads = [pltpu.make_async_copy(a, b, load_sem.at[i]) for i, (a, b) in enumerate(loads)]
    for copy in loads:
        copy.start()

    barrier = pltpu.get_barrier_semaphore()
    for peer in (right, left, sibling):
        pl.semaphore_signal(barrier, inc=1, device_id=(e, peer), device_id_type=MESH)

    def greet(i, carry):
        pl.semaphore_signal(
            barrier, inc=1, device_id=(lax.rem(e + i, ne), t), device_id_type=MESH
        )
        return carry

    lax.fori_loop(1, ne, greet, 0)

    loads[0].wait()
    loads[1].wait()
    loads[2].wait()
    named = [iota((ne, tok), 0) == rt[k : k + 1, :] for k in range(2)]
    earlier = flag(iota((tok, tok), 0) < iota((tok, tok), 1))
    before = dot(flag(named[0] | named[1]), earlier)
    target = [
        rt[k : k + 1, :].astype(F32) * rows8
        + jnp.sum(jnp.where(named[k], before, 0.0), axis=0, keepdims=True)
        for k in range(2)
    ]
    grad = og[...]
    row = iota((ne * rows8, tok), 0).astype(F32)
    rows = None
    for q in range(2):
        match = (row == target[0] + float(q * cap)) | (row == target[1] + float(q * cap))
        term = dot(flag(match), grad[:, q * half : (q + 1) * half])
        rows = term if rows is None else rows + term
    sent[...] = rows.reshape(ne, rows8, half).astype(BF16)

    def block(k, o, part=None):
        if part is None:
            return xt.at[k, pl.ds(pl.multiple_of(o * feat, 16), feat), :]
        return xt.at[k, pl.ds(pl.multiple_of(o * feat + part * half, 16), half), :]

    block(0, t)[...] = dot(grad, flag(iota((tok, lanes), 0) == iota((tok, lanes), 1)), TN).astype(
        BF16
    )
    small[...] = jnp.zeros_like(small)
    for k in range(2):
        small[k : k + 1, 0:tok] = target[k]
        small[2 + k : 3 + k, 0:tok] = cb[k : k + 1, :]

    pl.semaphore_wait(barrier, ne - 1 + 3)

    def ag_ring_copy(k, way, step, source):
        part = None if step < far - 1 else way
        ref = block(k, source * 2 + c, part)
        return pltpu.make_async_remote_copy(
            src_ref=ref,
            dst_ref=ref,
            send_sem=ag_send.at[k],
            recv_sem=ag_ring.at[k, way, step],
            device_id=(e, right if way == 0 else left),
            device_id_type=MESH,
        )

    def ag_pair_copy(k, index, source, core):
        ref = block(k, source * 2 + core)
        return pltpu.make_async_remote_copy(
            src_ref=ref,
            dst_ref=ref,
            send_sem=ag_send.at[k],
            recv_sem=ag_pair.at[k, index],
            device_id=(e, sibling),
            device_id_type=MESH,
        )

    def ag_start(k):
        ag_ring_copy(k, 0, 0, y).start()
        ag_ring_copy(k, 1, 0, y).start()
        ag_pair_copy(k, 0, y, c).start()

    def ag_step(k, step):
        ag_ring_copy(k, 0, step, ring_pos(-1 - step)).wait_recv()
        if step + 1 < far:
            ag_ring_copy(k, 0, step + 1, ring_pos(-1 - step)).start()
        ag_ring_copy(k, 1, step, ring_pos(1 + step)).wait_recv()
        if step + 1 < far:
            ag_ring_copy(k, 1, step + 1, ring_pos(1 + step)).start()
            ag_pair_copy(k, 2 * step + 1, ring_pos(-1 - step), c).start()
            ag_pair_copy(k, 2 * step + 2, ring_pos(1 + step), c).start()
        else:
            ag_pair_copy(k, 2 * step + 1, ring_pos(far), c).start()

    def ag_finish(k):
        ag_pair_copy(k, 0, y, 1 - c).wait_recv()
        for step in range(far - 1):
            ag_pair_copy(k, 2 * step + 1, ring_pos(-1 - step), 1 - c).wait_recv()
            ag_pair_copy(k, 2 * step + 2, ring_pos(1 + step), 1 - c).wait_recv()
        ag_pair_copy(k, 2 * far - 1, ring_pos(far), 1 - c).wait_recv()

    def hidden_grads(k, w, pre_gate, pre_up):
        hidden = dot(w_out[w], xt[k])
        gate = pre_gate.astype(F32)
        upper = pre_up.astype(F32)
        sig = jax.nn.sigmoid(gate)
        gate_grad = (hidden * upper * sig * (1.0 + gate * (1.0 - sig))).astype(BF16)
        up_grad = (hidden * gate * sig).astype(BF16)
        return gate_grad, up_grad

    def term(w, grads, o):
        at = pl.ds(pl.multiple_of(o * feat, 16), feat)
        return dot(w_in_t[w, 0, at, :], grads[0]) + dot(w_in_t[w, 1, at, :], grads[1])

    order = [far]
    for d in range(far - 1, 0, -1):
        order += [d, -d]
    order += [0]

    def rs_pair_copy(k, pos):
        return pltpu.make_async_remote_copy(
            src_ref=pair_out.at[k, pos],
            dst_ref=pair_in.at[k, pos],
            send_sem=rs_send.at[k, 0],
            recv_sem=rs_pair.at[k, pos],
            device_id=(e, sibling),
            device_id_type=MESH,
        )

    def rs_terms(k, w, grads):
        for d in order:
            pos = ring_pos(d)
            pair_out[k, pos] = term(w, grads, pos * 2 + (1 - c)).astype(BF16)
            rs_pair_copy(k, pos).start()
        for d in order:
            pos = ring_pos(d)
            own_part[k, pos] = term(w, grads, pos * 2 + c)

    def rs_ring_copy(k, way, step):
        at = pl.ds(0, feat) if step > 0 else pl.ds(way * half, half)
        return pltpu.make_async_remote_copy(
            src_ref=ring_out.at[k, way, step, at, :],
            dst_ref=ring_in.at[k, way, step, at, :],
            send_sem=rs_send.at[k, 1],
            recv_sem=rs_ring.at[k, way, step],
            device_id=(e, right if way == 0 else left),
            device_id_type=MESH,
        )

    def rs_start(k):
        pos = ring_pos(far)
        rs_pair_copy(k, pos).wait_recv()
        for way in range(2):
            at = pl.ds(way * half, half)
            ring_out[k, way, 0, at, :] = (
                own_part[k, pos, at, :] + pair_in[k, pos, at, :].astype(F32)
            ).astype(BF16)
            rs_ring_copy(k, way, 0).start()

    def rs_step(k, step):
        for way in range(2):
            pos = ring_pos(far - step if way == 0 else step - far)
            rs_pair_copy(k, pos).wait_recv()
            own = own_part[k, pos] + pair_in[k, pos].astype(F32)
            rs_ring_copy(k, way, step - 1).wait_recv()
            if step == 1:
                other = pl.ds((1 - way) * half, half)
                at = pl.ds(way * half, half)
                ring_out[k, way, 1, other, :] = own[(1 - way) * half : (2 - way) * half].astype(
                    BF16
                )
                ring_out[k, way, 1, at, :] = (
                    own[way * half : (1 + way) * half] + ring_in[k, way, 0, at, :].astype(F32)
                ).astype(BF16)
            else:
                ring_out[k, way, step] = (own + ring_in[k, way, step - 1].astype(F32)).astype(BF16)
            rs_ring_copy(k, way, step).start()

    def rs_end(k):
        rs_pair_copy(k, y).wait_recv()
        total = own_part[k, y] + pair_in[k, y].astype(F32)
        for way in range(2):
            rs_ring_copy(k, way, far - 1).wait_recv()
            total = total + ring_in[k, way, far - 1].astype(F32)
        return total

    def a2a_copy(d):
        return pltpu.make_async_remote_copy(
            src_ref=sent.at[d],
            dst_ref=arrived.at[e],
            send_sem=a2a_send,
            recv_sem=a2a_recv.at[lax.div(e, per)],
            device_id=(d, t),
            device_id_type=MESH,
        )

    def a2a_start(i, carry):
        a2a_copy(lax.rem(e + i, ne)).start()
        return carry

    def a2a_wait(h):
        ref = arrived.at[pl.ds(h * per, per)]
        pltpu.make_async_copy(ref, ref, a2a_recv.at[h]).wait()

    def select(q):
        n = iota((per * rows8, lanes), 1)
        r = iota((per * rows8, lanes), 0)
        return flag(r == lax.div(n, cap) * rows8 + q * cap + lax.rem(n, cap))

    def take_rows(h):
        rows = arrived[h * per : (h + 1) * per].astype(F32).reshape(per * rows8, half).astype(BF16)
        for q in range(2):
            block(1 + h, t, q)[...] = dot(rows, select(q), TN).astype(BF16)

    piece = min(256, nt * feat)
    pieces = nt * feat // piece

    def turn(w, first, last):
        eye = flag(iota((piece, piece), 0) == iota((piece, piece), 1))

        def one(j, carry):
            at = pl.ds(pl.multiple_of(j * piece, piece), piece)
            for m in range(2):
                w_in_t[w, m, at, :] = dot(eye, w_in[w, m, :, at], NT).astype(BF16)
            return carry

        lax.fori_loop(first, last, one, 0)

    cuts = [pieces * i // far for i in range(far + 1)]

    ag_start(0)
    pltpu.make_async_copy(sent.at[e], arrived.at[e], a2a_recv.at[lax.div(e, per)]).start()
    lax.fori_loop(1, ne, a2a_start, 0)
    loads[4].wait()
    for step in range(far):
        ag_step(0, step)
        turn(0, cuts[step], cuts[step + 1])
    for h in range(2):
        a2a_wait(h)
        take_rows(h)
        ag_start(1 + h)
    turned = small[...].T
    for k in range(2):
        for q in range(2):
            at = (2 * k + q) * tok
            picks[at : at + tok, :] = flag(
                iota((tok, ne * rows8), 1).astype(F32)
                == turned[0:tok, k : k + 1] + float(q * cap)
            )
    ag_finish(0)
    loads[3].wait()
    loads[5].wait()
    fill = jnp.zeros((units, lanes - tok), BF16)
    pre = [jnp.concatenate([pre_d[m], fill], axis=1) if lanes > tok else pre_d[m] for m in range(2)]
    rs_terms(0, 0, hidden_grads(0, 0, pre[0], pre[1]))
    rs_start(0)
    loads[7].wait()
    for step in range(far):
        ag_step(1, step)
        ag_step(2, step)
        if step + 1 < far:
            rs_step(0, step + 1)
        turn(1, cuts[step], cuts[step + 1])
    dense_sum[...] = rs_end(0).T
    loads[6].wait()
    loads[8].wait()
    for h in range(2):
        at = pl.ds(h * lanes, lanes)
        ag_finish(1 + h)
        rs_terms(1 + h, 1, hidden_grads(1 + h, 1, pre_e[0, :, at], pre_e[1, :, at]))
        rs_start(1 + h)
    for step in range(1, far):
        for h in range(2):
            rs_step(1 + h, step)

    for h in range(2):
        back = rs_end(1 + h).astype(BF16)
        rows = dot(select(0), back[0:half], NT) + dot(select(1), back[half:], NT)
        returning[h * per : (h + 1) * per] = rows.reshape(per, rows8, half).astype(BF16)

        def send_back(i, carry):
            d = h * per + lax.rem(e + i, per)

            @pl.when(d != e)
            def _():
                pltpu.make_async_remote_copy(
                    src_ref=returning.at[d],
                    dst_ref=returned.at[e],
                    send_sem=back_send,
                    recv_sem=back_recv,
                    device_id=(d, t),
                    device_id_type=MESH,
                ).start()

            @pl.when(d == e)
            def _():
                pltpu.make_async_copy(returning.at[d], returned.at[d], back_recv).start()

            return carry

        lax.fori_loop(0, per, send_back, 0)

    for k in range(3):
        ref = xt.at[k, pl.ds(0, (nt - 1) * feat), :]
        pltpu.make_async_copy(ref, ref, ag_send.at[k]).wait()
        pltpu.make_async_copy(pair_out.at[k], pair_out.at[k], rs_send.at[k, 0]).wait()
        ref = pair_out.at[k, pl.ds(0, ny - 1)]
        pltpu.make_async_copy(ref, ref, rs_send.at[k, 1]).wait()
    ref = sent.at[pl.ds(0, ne - 1)]
    pltpu.make_async_copy(ref, ref, a2a_send).wait()
    ref = returning.at[pl.ds(0, ne - 1)]
    pltpu.make_async_copy(ref, ref, back_send).wait()

    pltpu.make_async_copy(returned, returned, back_recv).wait()
    rows = returned[...].astype(F32).reshape(ne * rows8, half).astype(BF16)
    picked = dot(picks[...], rows)
    dense = dense_sum[...]
    for q in range(2):
        total = dense[0:tok, q * half : (q + 1) * half]
        for k in range(2):
            at = (2 * k + q) * tok
            total = total + turned[0:tok, 2 + k : 3 + k] * picked[at : at + tok]
        result[:, q * half : (q + 1) * half] = total.astype(BF16)


def local(
    out_grad, dense_pre, dense_in, dense_out, routes, combine, expert_pre, expert_in, expert_out
):
    ne = lax.axis_size("expert")
    nt = lax.axis_size("tensor")
    ny = nt // 2
    far = ny // 2
    tok, feat = out_grad.shape
    units = dense_out.shape[0]
    slots = expert_pre.shape[1]
    cap = slots // ne
    lanes = slots // 2
    rows8 = 2 * cap
    half = feat // 2
    dim = nt * feat
    sizes = (ne, ny, tok, feat, units, cap, lanes)
    dma = pltpu.SemaphoreType.DMA
    scratch = [
        pltpu.VMEM((tok, feat), BF16),
        pltpu.VMEM((2, tok), jnp.int32),
        pltpu.VMEM((2, tok), F32),
        pltpu.VMEM((2, units, tok), BF16),
        pltpu.VMEM((2, units, slots), BF16),
        pltpu.VMEM((2, units, dim), BF16),
        pltpu.VMEM((2, 2, units, dim), BF16),
        pltpu.VMEM((2, 2, dim, units), BF16),
        pltpu.VMEM((8, 128), F32),
        pltpu.VMEM((4 * tok, ne * rows8), BF16),
        pltpu.VMEM((ne, rows8, half), BF16),
        pltpu.VMEM((ne, rows8, half), BF16),
        pltpu.VMEM((ne, rows8, half), BF16),
        pltpu.VMEM((ne, rows8, half), BF16),
        pltpu.VMEM((3, dim, lanes), BF16),
        pltpu.VMEM((3, ny, feat, lanes), F32),
        pltpu.VMEM((3, ny, feat, lanes), BF16),
        pltpu.VMEM((3, ny, feat, lanes), BF16),
        pltpu.VMEM((3, 2, far, feat, lanes), BF16),
        pltpu.VMEM((3, 2, far, feat, lanes), BF16),
        pltpu.VMEM((lanes, feat), F32),
        dma((9,)),
        dma,
        dma((2,)),
        dma,
        dma,
        dma((3,)),
        dma((3, 2, far)),
        dma((3, ny)),
        dma((3, 2)),
        dma((3, 2, far)),
        dma((3, ny)),
    ]
    any_spec = pl.BlockSpec(memory_space=pl.ANY)
    return pl.pallas_call(
        functools.partial(kernel, sizes),
        out_shape=jax.ShapeDtypeStruct((tok, feat), BF16),
        in_specs=[any_spec] * 9,
        out_specs=pl.BlockSpec(memory_space=pltpu.VMEM),
        scratch_shapes=scratch,
        compiler_params=pltpu.CompilerParams(
            collective_id=0, has_side_effects=True, vmem_limit_bytes=56 * 1024 * 1024
        ),
    )(
        out_grad,
        routes.T,
        combine.T,
        dense_pre.transpose(1, 2, 0),
        expert_pre[0].transpose(1, 2, 0),
        dense_out,
        dense_in,
        expert_out[0],
        expert_in[0],
    )


def solution(mesh):
    return jax.shard_map(
        local,
        mesh=mesh,
        in_specs=(
            P("expert", "tensor"),
            P("expert", None, "tensor"),
            P(None, "tensor", None),
            P("tensor", None),
            P("expert", None),
            P("expert", None),
            P("expert", None, None, "tensor"),
            P("expert", None, "tensor", None),
            P("expert", "tensor", None),
        ),
        out_specs=P("expert", "tensor"),
        check_vma=False,
    )
```

```python
import functools

import jax
import jax.numpy as jnp
from jax import lax
from jax.experimental import pallas as pl
from jax.experimental.pallas import tpu as pltpu
from jax.sharding import PartitionSpec as P

BF16 = jnp.bfloat16
F32 = jnp.float32
MESH = pl.DeviceIdType.MESH
TN = (((0,), (0,)), ((), ()))
NT = (((1,), (1,)), ((), ()))


def dot(a, b, dims=(((1,), (0,)), ((), ()))):
    return lax.dot_general(a, b, dims, preferred_element_type=F32)


def iota(shape, dim):
    return lax.broadcasted_iota(jnp.int32, shape, dim)


def flag(mask):
    return jnp.where(mask, 1.0, 0.0).astype(BF16)


def kernel(
    sizes,
    og_hbm,
    rt_hbm,
    cb_hbm,
    pre_d_hbm,
    pre_e_hbm,
    out_d_hbm,
    in_d_hbm,
    out_e_hbm,
    in_e_hbm,
    result,
    og,
    rt,
    cb,
    pre_d,
    pre_e,
    w_out,
    w_in,
    w_in_t,
    small,
    picks,
    sent,
    arrived,
    returning,
    returned,
    xt,
    own_part,
    pair_out,
    pair_in,
    ring_out,
    ring_in,
    dense_sum,
    load_sem,
    a2a_send,
    a2a_recv,
    back_send,
    back_recv,
    ag_send,
    ag_ring,
    ag_pair,
    ag_cross,
    rs_send,
    rs_ring,
    rs_pair,
):
    ne, ny, tok, feat, units, cap, lanes = sizes
    nt = 2 * ny
    far = ny // 2
    half = feat // 2
    rows8 = 2 * cap
    per = ne // 2
    e = lax.axis_index("expert")
    t = lax.axis_index("tensor")
    y = lax.div(t, 2)
    c = lax.rem(t, 2)
    right = lax.rem(y + 1, ny) * 2 + c
    left = lax.rem(y + ny - 1, ny) * 2 + c
    sibling = y * 2 + (1 - c)

    def ring_pos(offset):
        return lax.rem(y + (offset + 2 * ny), ny)

    loads = [
        (rt_hbm, rt),
        (og_hbm, og),
        (cb_hbm, cb),
        (out_d_hbm, w_out.at[0]),
        (in_d_hbm, w_in.at[0]),
        (pre_d_hbm, pre_d),
        (out_e_hbm, w_out.at[1]),
        (in_e_hbm, w_in.at[1]),
        (pre_e_hbm, pre_e),
    ]
    loads = [pltpu.make_async_copy(a, b, load_sem.at[i]) for i, (a, b) in enumerate(loads)]
    for copy in loads:
        copy.start()

    barrier = pltpu.get_barrier_semaphore()
    across = [right + 1 - 2 * c, left + 1 - 2 * c]
    for peer in (right, left, sibling, across[0], across[1]):
        pl.semaphore_signal(barrier, inc=1, device_id=(e, peer), device_id_type=MESH)

    def outward(start, i):
        return start + jnp.where(lax.rem(i, 2) == 1, -lax.div(i + 1, 2), lax.div(i, 2))

    def greet(i, carry):
        d = lax.rem(outward(e + ne // 2, i) + ne, ne)
        pl.semaphore_signal(barrier, inc=1, device_id=(d, t), device_id_type=MESH)
        return carry

    lax.fori_loop(0, ne - 1, greet, 0)

    loads[0].wait()
    loads[1].wait()
    loads[2].wait()
    named = [iota((ne, tok), 0) == rt[k : k + 1, :] for k in range(2)]
    earlier = flag(iota((tok, tok), 0) < iota((tok, tok), 1))
    before = dot(flag(named[0] | named[1]), earlier)
    target = [
        rt[k : k + 1, :].astype(F32) * rows8
        + jnp.sum(jnp.where(named[k], before, 0.0), axis=0, keepdims=True)
        for k in range(2)
    ]
    grad = og[...]
    row = iota((ne * rows8, tok), 0).astype(F32)
    rows = None
    for q in range(2):
        match = (row == target[0] + float(q * cap)) | (row == target[1] + float(q * cap))
        term = dot(flag(match), grad[:, q * half : (q + 1) * half])
        rows = term if rows is None else rows + term
    sent[...] = rows.reshape(ne, rows8, half).astype(BF16)

    def block(k, o, part=None):
        if part is None:
            return xt.at[k, pl.ds(pl.multiple_of(o * feat, 16), feat), :]
        return xt.at[k, pl.ds(pl.multiple_of(o * feat + part * half, 16), half), :]

    block(0, t)[...] = dot(grad, flag(iota((tok, lanes), 0) == iota((tok, lanes), 1)), TN).astype(
        BF16
    )
    small[...] = jnp.zeros_like(small)
    for k in range(2):
        small[k : k + 1, 0:tok] = target[k]
        small[2 + k : 3 + k, 0:tok] = cb[k : k + 1, :]

    pl.semaphore_wait(barrier, ne - 1 + 5)

    def ag_ring_copy(k, way, step, source):
        part = None if step < far - 1 else way
        ref = block(k, source * 2 + c, part)
        return pltpu.make_async_remote_copy(
            src_ref=ref,
            dst_ref=ref,
            send_sem=ag_send.at[k],
            recv_sem=ag_ring.at[k, way, step],
            device_id=(e, right if way == 0 else left),
            device_id_type=MESH,
        )

    def ag_pair_copy(k, index, source, core):
        ref = block(k, source * 2 + core)
        return pltpu.make_async_remote_copy(
            src_ref=ref,
            dst_ref=ref,
            send_sem=ag_send.at[k],
            recv_sem=ag_pair.at[k, index],
            device_id=(e, sibling),
            device_id_type=MESH,
        )

    def ag_cross_copy(k, way, source, core):
        ref = block(k, source * 2 + core, way)
        return pltpu.make_async_remote_copy(
            src_ref=ref,
            dst_ref=ref,
            send_sem=ag_send.at[k],
            recv_sem=ag_cross.at[k, way],
            device_id=(e, across[way]),
            device_id_type=MESH,
        )

    def ag_start(k):
        ag_ring_copy(k, 0, 0, y).start()
        ag_ring_copy(k, 1, 0, y).start()
        ag_pair_copy(k, 0, y, c).start()

    def ag_step(k, step):
        for way in range(2):
            source = ring_pos(-1 - step if way == 0 else 1 + step)
            ag_ring_copy(k, way, step, source).wait_recv()
            if step + 1 < far:
                ag_ring_copy(k, way, step + 1, source).start()
            if step + 2 == far:
                ag_cross_copy(k, way, source, c).start()
        if step + 1 < far:
            ag_pair_copy(k, 2 * step + 1, ring_pos(-1 - step), c).start()
            ag_pair_copy(k, 2 * step + 2, ring_pos(1 + step), c).start()

    def ag_finish(k):
        ag_pair_copy(k, 0, y, 1 - c).wait_recv()
        for step in range(far - 1):
            ag_pair_copy(k, 2 * step + 1, ring_pos(-1 - step), 1 - c).wait_recv()
            ag_pair_copy(k, 2 * step + 2, ring_pos(1 + step), 1 - c).wait_recv()
        for way in range(2):
            ag_cross_copy(k, way, ring_pos(far), 1 - c).wait_recv()

    def hidden_grads(w, x, pre_gate, pre_up):
        hidden = dot(w_out[w], x)
        gate = pre_gate.astype(F32)
        upper = pre_up.astype(F32)
        sig = jax.nn.sigmoid(gate)
        gate_grad = (hidden * upper * sig * (1.0 + gate * (1.0 - sig))).astype(BF16)
        up_grad = (hidden * gate * sig).astype(BF16)
        return gate_grad, up_grad

    order = [far]
    for d in range(far - 1, 0, -1):
        order += [d, -d]
    order += [0]

    def rs_pair_copy(k, pos):
        return pltpu.make_async_remote_copy(
            src_ref=pair_out.at[k, pos],
            dst_ref=pair_in.at[k, pos],
            send_sem=rs_send.at[k, 0],
            recv_sem=rs_pair.at[k, pos],
            device_id=(e, sibling),
            device_id_type=MESH,
        )

    def rs_terms(w, chunks, grads, d):
        pos = ring_pos(d)
        at = pl.ds(pl.multiple_of(pos * (2 * feat), 16), 2 * feat)
        both = dot(w_in_t[w, 0, at, :], grads[0]) + dot(w_in_t[w, 1, at, :], grads[1])
        other = lax.select(c == 0, both[feat:], both[:feat]).astype(BF16)
        own = lax.select(c == 0, both[:feat], both[feat:])
        for i, k in enumerate(chunks):
            pair_out[k, pos] = other[:, i * lanes : (i + 1) * lanes]
            rs_pair_copy(k, pos).start()
            own_part[k, pos] = own[:, i * lanes : (i + 1) * lanes]

    def rs_ring_copy(k, way, step):
        at = pl.ds(0, feat) if step > 0 else pl.ds(way * half, half)
        return pltpu.make_async_remote_copy(
            src_ref=ring_out.at[k, way, step, at, :],
            dst_ref=ring_in.at[k, way, step, at, :],
            send_sem=rs_send.at[k, 1],
            recv_sem=rs_ring.at[k, way, step],
            device_id=(e, right if way == 0 else left),
            device_id_type=MESH,
        )

    def rs_start(k):
        pos = ring_pos(far)
        rs_pair_copy(k, pos).wait_recv()
        for way in range(2):
            at = pl.ds(way * half, half)
            ring_out[k, way, 0, at, :] = (
                own_part[k, pos, at, :] + pair_in[k, pos, at, :].astype(F32)
            ).astype(BF16)
            rs_ring_copy(k, way, 0).start()

    def rs_step(k, step):
        for way in range(2):
            pos = ring_pos(far - step if way == 0 else step - far)
            rs_pair_copy(k, pos).wait_recv()
            own = own_part[k, pos] + pair_in[k, pos].astype(F32)
            rs_ring_copy(k, way, step - 1).wait_recv()
            if step == 1:
                other = pl.ds((1 - way) * half, half)
                at = pl.ds(way * half, half)
                ring_out[k, way, 1, other, :] = own[(1 - way) * half : (2 - way) * half].astype(
                    BF16
                )
                ring_out[k, way, 1, at, :] = (
                    own[way * half : (1 + way) * half] + ring_in[k, way, 0, at, :].astype(F32)
                ).astype(BF16)
            else:
                ring_out[k, way, step] = (own + ring_in[k, way, step - 1].astype(F32)).astype(BF16)
            rs_ring_copy(k, way, step).start()

    def rs_end(k):
        rs_pair_copy(k, y).wait_recv()
        total = own_part[k, y] + pair_in[k, y].astype(F32)
        for way in range(2):
            rs_ring_copy(k, way, far - 1).wait_recv()
            total = total + ring_in[k, way, far - 1].astype(F32)
        return total

    def a2a_copy(d):
        return pltpu.make_async_remote_copy(
            src_ref=sent.at[d],
            dst_ref=arrived.at[e],
            send_sem=a2a_send,
            recv_sem=a2a_recv.at[lax.div(e, per)],
            device_id=(d, t),
            device_id_type=MESH,
        )

    def a2a_start(i, carry):
        a2a_copy(lax.rem(outward(e + ne // 2, i) + ne, ne)).start()
        return carry

    def a2a_wait(h):
        ref = arrived.at[pl.ds(h * per, per)]
        pltpu.make_async_copy(ref, ref, a2a_recv.at[h]).wait()

    def select(q):
        n = iota((per * rows8, lanes), 1)
        r = iota((per * rows8, lanes), 0)
        return flag(r == lax.div(n, cap) * rows8 + q * cap + lax.rem(n, cap))

    def take_rows(h):
        rows = arrived[h * per : (h + 1) * per].astype(F32).reshape(per * rows8, half).astype(BF16)
        for q in range(2):
            block(1 + h, t, q)[...] = dot(rows, select(q), TN).astype(BF16)

    piece = min(256, nt * feat)
    pieces = nt * feat // piece

    def turn(w, first, last):
        eye = flag(iota((piece, piece), 0) == iota((piece, piece), 1))

        def one(j, carry):
            at = pl.ds(pl.multiple_of(j * piece, piece), piece)
            for m in range(2):
                w_in_t[w, m, at, :] = dot(eye, w_in[w, m, :, at], NT).astype(BF16)
            return carry

        lax.fori_loop(first, last, one, 0)

    ag_start(0)
    pltpu.make_async_copy(sent.at[e], arrived.at[e], a2a_recv.at[lax.div(e, per)]).start()
    lax.fori_loop(0, ne - 1, a2a_start, 0)
    loads[4].wait()
    turn(0, 0, pieces // 2)
    ag_step(0, 0)
    turn(0, pieces // 2, pieces)
    ag_step(0, 1)
    loads[7].wait()
    turn(1, 0, pieces // 2)
    for step in range(2, far - 1):
        ag_step(0, step)
    turn(1, pieces // 2, pieces)
    for i in (3, 5, 6, 8):
        loads[i].wait()
    for h in range(2):
        a2a_wait(h)
        take_rows(h)
        ag_start(1 + h)
    for step in range(max(2, far - 1), far):
        ag_step(0, step)
    fill = jnp.zeros((units, lanes - tok), BF16)
    pre = [jnp.concatenate([pre_d[m], fill], axis=1) if lanes > tok else pre_d[m] for m in range(2)]
    groups = [order[: ny // 2], order[ny // 2 :]]
    grads = None
    for step in range(far):
        for k in (1, 2):
            ag_step(k, step)
        if step == 0:
            ag_finish(0)
            grads = hidden_grads(0, xt[0], pre[0], pre[1])
        elif groups:
            for d in groups.pop(0):
                rs_terms(0, (0,), grads, d)
    for group in groups:
        for d in group:
            rs_terms(0, (0,), grads, d)
    rs_start(0)
    for k in (1, 2):
        ag_finish(k)
    grads = hidden_grads(1, jnp.concatenate([xt[1], xt[2]], axis=1), pre_e[0], pre_e[1])
    for d in order[:3]:
        rs_terms(1, (1, 2), grads, d)
    for k in (1, 2):
        rs_start(k)
    rs_step(0, 1)
    for d in order[3:]:
        rs_terms(1, (1, 2), grads, d)
    for step in range(1, far):
        for k in (1, 2):
            rs_step(k, step)
        if step + 1 < far:
            rs_step(0, step + 1)

    for h in range(2):
        back = rs_end(1 + h).astype(BF16)
        rows = dot(select(0), back[0:half], NT) + dot(select(1), back[half:], NT)
        returning[h * per : (h + 1) * per] = rows.reshape(per, rows8, half).astype(BF16)

        def send_back(i, carry):
            near = jnp.where(lax.div(e, per) == h, per // 2, 0)
            d = h * per + lax.rem(outward(e + near, i) + ne, per)

            @pl.when(d != e)
            def _():
                pltpu.make_async_remote_copy(
                    src_ref=returning.at[d],
                    dst_ref=returned.at[e],
                    send_sem=back_send,
                    recv_sem=back_recv,
                    device_id=(d, t),
                    device_id_type=MESH,
                ).start()

            @pl.when(d == e)
            def _():
                pltpu.make_async_copy(returning.at[d], returned.at[d], back_recv).start()

            return carry

        lax.fori_loop(0, per, send_back, 0)

    turned = small[...].T
    for k in range(2):
        for q in range(2):
            at = (2 * k + q) * tok
            picks[at : at + tok, :] = flag(
                iota((tok, ne * rows8), 1).astype(F32)
                == turned[0:tok, k : k + 1] + float(q * cap)
            )
    dense_sum[...] = rs_end(0).T

    for k in range(3):
        ref = xt.at[k, pl.ds(0, (nt - 1) * feat), :]
        pltpu.make_async_copy(ref, ref, ag_send.at[k]).wait()
        pltpu.make_async_copy(pair_out.at[k], pair_out.at[k], rs_send.at[k, 0]).wait()
        ref = pair_out.at[k, pl.ds(0, ny - 1)]
        pltpu.make_async_copy(ref, ref, rs_send.at[k, 1]).wait()
    ref = sent.at[pl.ds(0, ne - 1)]
    pltpu.make_async_copy(ref, ref, a2a_send).wait()
    ref = returning.at[pl.ds(0, ne - 1)]
    pltpu.make_async_copy(ref, ref, back_send).wait()

    pltpu.make_async_copy(returned, returned, back_recv).wait()
    rows = returned[...].astype(F32).reshape(ne * rows8, half).astype(BF16)
    picked = dot(picks[...], rows)
    dense = dense_sum[...]
    for q in range(2):
        total = dense[0:tok, q * half : (q + 1) * half]
        for k in range(2):
            at = (2 * k + q) * tok
            total = total + turned[0:tok, 2 + k : 3 + k] * picked[at : at + tok]
        result[:, q * half : (q + 1) * half] = total.astype(BF16)


def local(
    out_grad, dense_pre, dense_in, dense_out, routes, combine, expert_pre, expert_in, expert_out
):
    ne = lax.axis_size("expert")
    nt = lax.axis_size("tensor")
    ny = nt // 2
    far = ny // 2
    tok, feat = out_grad.shape
    units = dense_out.shape[0]
    slots = expert_pre.shape[1]
    cap = slots // ne
    lanes = slots // 2
    rows8 = 2 * cap
    half = feat // 2
    dim = nt * feat
    sizes = (ne, ny, tok, feat, units, cap, lanes)
    dma = pltpu.SemaphoreType.DMA
    scratch = [
        pltpu.VMEM((tok, feat), BF16),
        pltpu.VMEM((2, tok), jnp.int32),
        pltpu.VMEM((2, tok), F32),
        pltpu.VMEM((2, units, tok), BF16),
        pltpu.VMEM((2, units, slots), BF16),
        pltpu.VMEM((2, units, dim), BF16),
        pltpu.VMEM((2, 2, units, dim), BF16),
        pltpu.VMEM((2, 2, dim, units), BF16),
        pltpu.VMEM((8, 128), F32),
        pltpu.VMEM((4 * tok, ne * rows8), BF16),
        pltpu.VMEM((ne, rows8, half), BF16),
        pltpu.VMEM((ne, rows8, half), BF16),
        pltpu.VMEM((ne, rows8, half), BF16),
        pltpu.VMEM((ne, rows8, half), BF16),
        pltpu.VMEM((3, dim, lanes), BF16),
        pltpu.VMEM((3, ny, feat, lanes), F32),
        pltpu.VMEM((3, ny, feat, lanes), BF16),
        pltpu.VMEM((3, ny, feat, lanes), BF16),
        pltpu.VMEM((3, 2, far, feat, lanes), BF16),
        pltpu.VMEM((3, 2, far, feat, lanes), BF16),
        pltpu.VMEM((lanes, feat), F32),
        dma((9,)),
        dma,
        dma((2,)),
        dma,
        dma,
        dma((3,)),
        dma((3, 2, far)),
        dma((3, ny)),
        dma((3, 2)),
        dma((3, 2)),
        dma((3, 2, far)),
        dma((3, ny)),
    ]
    any_spec = pl.BlockSpec(memory_space=pl.ANY)
    return pl.pallas_call(
        functools.partial(kernel, sizes),
        out_shape=pltpu.VMEM((tok, feat), BF16),
        in_specs=[any_spec] * 9,
        out_specs=pl.BlockSpec(memory_space=pltpu.VMEM),
        scratch_shapes=scratch,
        compiler_params=pltpu.CompilerParams(
            collective_id=0, has_side_effects=True, vmem_limit_bytes=56 * 1024 * 1024
        ),
    )(
        out_grad,
        routes.T,
        combine.T,
        dense_pre.transpose(1, 2, 0),
        expert_pre[0].transpose(1, 2, 0),
        dense_out,
        dense_in,
        expert_out[0],
        expert_in[0],
    )


def solution(mesh):
    return jax.shard_map(
        local,
        mesh=mesh,
        in_specs=(
            P("expert", "tensor"),
            P("expert", None, "tensor"),
            P(None, "tensor", None),
            P("tensor", None),
            P("expert", None),
            P("expert", None),
            P("expert", None, None, "tensor"),
            P("expert", None, "tensor", None),
            P("expert", "tensor", None),
        ),
        out_specs=P("expert", "tensor"),
        check_vma=False,
    )
```

```python
import functools

import jax
import jax.numpy as jnp
from jax import lax
from jax.experimental import pallas as pl
from jax.experimental.pallas import tpu as pltpu
from jax.sharding import PartitionSpec as P

BF16 = jnp.bfloat16
F32 = jnp.float32
MESH = pl.DeviceIdType.MESH
TN = (((0,), (0,)), ((), ()))
NT = (((1,), (1,)), ((), ()))


def dot(a, b, dims=(((1,), (0,)), ((), ()))):
    return lax.dot_general(a, b, dims, preferred_element_type=F32)


def iota(shape, dim):
    return lax.broadcasted_iota(jnp.int32, shape, dim)


def flag(mask):
    return jnp.where(mask, 1.0, 0.0).astype(BF16)


def kernel(
    sizes,
    og_hbm,
    rt_hbm,
    cb_hbm,
    pre_d_hbm,
    pre_e_hbm,
    out_d_hbm,
    in_d_hbm,
    out_e_hbm,
    in_e_hbm,
    result,
    og,
    rt,
    cb,
    pre_d,
    pre_e,
    w_out,
    w_in,
    w_in_t,
    small,
    picks,
    select,
    sent,
    arrived,
    returning,
    returned,
    xt,
    own_part,
    pair_out,
    pair_in,
    ring_out,
    ring_in,
    dense_sum,
    load_sem,
    a2a_send,
    a2a_recv,
    back_send,
    back_recv,
    ag_send,
    ag_ring,
    ag_pair,
    ag_cross,
    rs_send,
    rs_ring,
    rs_pair,
):
    ne, ny, tok, feat, units, cap, lanes = sizes
    nt = 2 * ny
    far = ny // 2
    half = feat // 2
    rows8 = 2 * cap
    per = ne // 2
    e = lax.axis_index("expert")
    t = lax.axis_index("tensor")
    y = lax.div(t, 2)
    c = lax.rem(t, 2)
    right = lax.rem(y + 1, ny) * 2 + c
    left = lax.rem(y + ny - 1, ny) * 2 + c
    sibling = y * 2 + (1 - c)

    def ring_pos(offset):
        return lax.rem(y + (offset + 2 * ny), ny)

    loads = [
        (rt_hbm, rt),
        (og_hbm, og),
        (cb_hbm, cb),
        (out_d_hbm, w_out.at[0]),
        (in_d_hbm, w_in.at[0]),
        (pre_d_hbm, pre_d),
        (out_e_hbm, w_out.at[1]),
        (in_e_hbm, w_in.at[1]),
        (pre_e_hbm, pre_e),
    ]
    loads = [pltpu.make_async_copy(a, b, load_sem.at[i]) for i, (a, b) in enumerate(loads)]
    for copy in loads:
        copy.start()

    barrier = pltpu.get_barrier_semaphore()
    across = [right + 1 - 2 * c, left + 1 - 2 * c]
    for peer in (right, left, sibling, across[0], across[1]):
        pl.semaphore_signal(barrier, inc=1, device_id=(e, peer), device_id_type=MESH)

    def outward(start, i):
        return start + jnp.where(lax.rem(i, 2) == 1, -lax.div(i + 1, 2), lax.div(i, 2))

    def greet(i, carry):
        d = lax.rem(outward(e + ne // 2, i) + ne, ne)
        pl.semaphore_signal(barrier, inc=1, device_id=(d, t), device_id_type=MESH)
        return carry

    lax.fori_loop(0, ne - 1, greet, 0)

    loads[0].wait()
    loads[1].wait()
    loads[2].wait()
    named = [iota((ne, tok), 0) == rt[k : k + 1, :] for k in range(2)]
    earlier = flag(iota((tok, tok), 0) < iota((tok, tok), 1))
    before = dot(flag(named[0] | named[1]), earlier)
    target = [
        rt[k : k + 1, :].astype(F32) * rows8
        + jnp.sum(jnp.where(named[k], before, 0.0), axis=0, keepdims=True)
        for k in range(2)
    ]
    grad = og[...]
    row = iota((ne * rows8, tok), 0).astype(F32)
    rows = None
    for q in range(2):
        match = (row == target[0] + float(q * cap)) | (row == target[1] + float(q * cap))
        term = dot(flag(match), grad[:, q * half : (q + 1) * half])
        rows = term if rows is None else rows + term
    sent[...] = rows.reshape(ne, rows8, half).astype(BF16)

    def block(k, o, part=None):
        if part is None:
            return xt.at[k, pl.ds(pl.multiple_of(o * feat, 16), feat), :]
        return xt.at[k, pl.ds(pl.multiple_of(o * feat + part * half, 16), half), :]

    block(0, t)[...] = dot(grad, flag(iota((tok, lanes), 0) == iota((tok, lanes), 1)), TN).astype(
        BF16
    )
    small[...] = jnp.zeros_like(small)
    for k in range(2):
        small[k : k + 1, 0:tok] = target[k]
        small[2 + k : 3 + k, 0:tok] = cb[k : k + 1, :]

    pl.semaphore_wait(barrier, ne - 1 + 5)

    def ag_ring_copy(k, way, step, part, source):
        ref = block(k, source * 2 + c, part)
        return pltpu.make_async_remote_copy(
            src_ref=ref,
            dst_ref=ref,
            send_sem=ag_send.at[k],
            recv_sem=ag_ring.at[k, way, step, part],
            device_id=(e, right if way == 0 else left),
            device_id_type=MESH,
        )

    def ag_pair_copy(k, index, source, core):
        ref = block(k, source * 2 + core)
        return pltpu.make_async_remote_copy(
            src_ref=ref,
            dst_ref=ref,
            send_sem=ag_send.at[k],
            recv_sem=ag_pair.at[k, index],
            device_id=(e, sibling),
            device_id_type=MESH,
        )

    def ag_cross_copy(k, way, source, core):
        ref = block(k, source * 2 + core, way)
        return pltpu.make_async_remote_copy(
            src_ref=ref,
            dst_ref=ref,
            send_sem=ag_send.at[k],
            recv_sem=ag_cross.at[k, way],
            device_id=(e, across[way]),
            device_id_type=MESH,
        )

    def ag_start(k):
        for i in range(2):
            for way in range(2):
                ag_ring_copy(k, way, 0, i if way == 0 else 1 - i, y).start()
        ag_pair_copy(k, 0, y, c).start()

    def ag_step(chunks, step):
        for k in chunks:
            for i in range(2 if step + 1 < far else 1):
                for way in range(2):
                    part = i if way == 0 else 1 - i
                    source = ring_pos(-1 - step if way == 0 else 1 + step)
                    ag_ring_copy(k, way, step, part, source).wait_recv()
                    if step + 2 < far or (step + 2 == far and i == 0):
                        ag_ring_copy(k, way, step + 1, part, source).start()
                    if step + 2 == far and i == 0:
                        ag_cross_copy(k, way, source, c).start()
        if step + 1 < far:
            for k in chunks:
                ag_pair_copy(k, 2 * step + 1, ring_pos(-1 - step), c).start()
                ag_pair_copy(k, 2 * step + 2, ring_pos(1 + step), c).start()

    def ag_finish(k):
        ag_pair_copy(k, 0, y, 1 - c).wait_recv()
        for step in range(far - 1):
            ag_pair_copy(k, 2 * step + 1, ring_pos(-1 - step), 1 - c).wait_recv()
            ag_pair_copy(k, 2 * step + 2, ring_pos(1 + step), 1 - c).wait_recv()
        for way in range(2):
            ag_cross_copy(k, way, ring_pos(far), 1 - c).wait_recv()

    def hidden_grads(w, x, pre_gate, pre_up):
        hidden = dot(w_out[w], x)
        gate = pre_gate.astype(F32)
        upper = pre_up.astype(F32)
        sig = jax.nn.sigmoid(gate)
        gate_grad = (hidden * upper * sig * (1.0 + gate * (1.0 - sig))).astype(BF16)
        up_grad = (hidden * gate * sig).astype(BF16)
        return gate_grad, up_grad

    order = [far]
    for d in range(far - 1, 0, -1):
        order += [d, -d]
    order += [0]

    def rs_pair_copy(k, pos):
        return pltpu.make_async_remote_copy(
            src_ref=pair_out.at[k, pos],
            dst_ref=pair_in.at[k, pos],
            send_sem=rs_send.at[k, 0],
            recv_sem=rs_pair.at[k, pos],
            device_id=(e, sibling),
            device_id_type=MESH,
        )

    def rs_terms(w, chunks, grads, d):
        pos = ring_pos(d)
        at = pl.ds(pl.multiple_of(pos * (2 * feat), 16), 2 * feat)
        both = dot(w_in_t[w, 0, at, :], grads[0]) + dot(w_in_t[w, 1, at, :], grads[1])
        other = lax.select(c == 0, both[feat:], both[:feat]).astype(BF16)
        own = lax.select(c == 0, both[:feat], both[feat:])
        for i, k in enumerate(chunks):
            pair_out[k, pos] = other[:, i * lanes : (i + 1) * lanes]
            rs_pair_copy(k, pos).start()
            own_part[k, pos] = own[:, i * lanes : (i + 1) * lanes]

    def rs_ring_copy(k, way, step, part):
        at = pl.ds(part * half, half)
        return pltpu.make_async_remote_copy(
            src_ref=ring_out.at[k, way, step, at, :],
            dst_ref=ring_in.at[k, way, step, at, :],
            send_sem=rs_send.at[k, 1],
            recv_sem=rs_ring.at[k, way, step, part],
            device_id=(e, right if way == 0 else left),
            device_id_type=MESH,
        )

    def rs_send_on(k, way, step, part, pos, add):
        at = pl.ds(part * half, half)
        total = own_part[k, pos, at, :] + pair_in[k, pos, at, :].astype(F32)
        if add:
            rs_ring_copy(k, way, step - 1, part).wait_recv()
            total = total + ring_in[k, way, step - 1, at, :].astype(F32)
        ring_out[k, way, step, at, :] = total.astype(BF16)
        rs_ring_copy(k, way, step, part).start()

    def rs_start(k):
        rs_pair_copy(k, ring_pos(far)).wait_recv()
        for way in range(2):
            rs_send_on(k, way, 0, way, ring_pos(far), False)

    def rs_step(k, step):
        spots = [ring_pos(far - step), ring_pos(step - far)]
        for way in range(2):
            rs_pair_copy(k, spots[way]).wait_recv()
        for i in range(2):
            for way in range(2):
                part = 1 - way if i == 0 else way
                rs_send_on(k, way, step, part, spots[way], step > 1 or part == way)

    def rs_end(k):
        rs_pair_copy(k, y).wait_recv()
        total = own_part[k, y] + pair_in[k, y].astype(F32)
        for way in range(2):
            for part in range(2):
                rs_ring_copy(k, way, far - 1, part).wait_recv()
            total = total + ring_in[k, way, far - 1].astype(F32)
        return total

    def a2a_copy(d):
        return pltpu.make_async_remote_copy(
            src_ref=sent.at[d],
            dst_ref=arrived.at[e],
            send_sem=a2a_send,
            recv_sem=a2a_recv.at[lax.div(e, per)],
            device_id=(d, t),
            device_id_type=MESH,
        )

    def a2a_start(i, carry):
        a2a_copy(lax.rem(outward(e + ne // 2, i) + ne, ne)).start()
        return carry

    def a2a_wait(h):
        ref = arrived.at[pl.ds(h * per, per)]
        pltpu.make_async_copy(ref, ref, a2a_recv.at[h]).wait()

    def fill_select(q):
        n = iota((per * rows8, lanes), 1)
        r = iota((per * rows8, lanes), 0)
        select[q] = flag(r == lax.div(n, cap) * rows8 + q * cap + lax.rem(n, cap))

    def take_rows(h):
        rows = arrived[h * per : (h + 1) * per].astype(F32).reshape(per * rows8, half).astype(BF16)
        for q in range(2):
            block(1 + h, t, q)[...] = dot(rows, select[q], TN).astype(BF16)

    piece = min(256, nt * feat)
    pieces = nt * feat // piece

    def turn(w, first, last):
        eye = flag(iota((piece, piece), 0) == iota((piece, piece), 1))

        def one(j, carry):
            at = pl.ds(pl.multiple_of(j * piece, piece), piece)
            for m in range(2):
                w_in_t[w, m, at, :] = dot(eye, w_in[w, m, :, at], NT).astype(BF16)
            return carry

        lax.fori_loop(first, last, one, 0)

    ag_start(0)
    pltpu.make_async_copy(sent.at[e], arrived.at[e], a2a_recv.at[lax.div(e, per)]).start()
    lax.fori_loop(0, ne - 1, a2a_start, 0)
    loads[4].wait()
    for q in range(2):
        fill_select(q)
    turn(0, 0, pieces // 2)
    ag_step((0,), 0)
    turn(0, pieces // 2, pieces)
    ag_step((0,), 1)
    loads[7].wait()
    turn(1, 0, pieces // 2)
    for step in range(2, far - 1):
        ag_step((0,), step)
    turn(1, pieces // 2, pieces)
    for i in (3, 5, 6, 8):
        loads[i].wait()
    for h in range(2):
        a2a_wait(h)
        take_rows(h)
        ag_start(1 + h)
    for step in range(max(2, far - 1), far):
        ag_step((0,), step)
    ag_finish(0)
    fill = jnp.zeros((units, lanes - tok), BF16)
    pre = [jnp.concatenate([pre_d[m], fill], axis=1) if lanes > tok else pre_d[m] for m in range(2)]
    grads = hidden_grads(0, xt[0], pre[0], pre[1])
    for d in order[:2]:
        rs_terms(0, (0,), grads, d)
    for step in range(far):
        ag_step((1, 2), step)
        if step == 0:
            for d in order[2:]:
                rs_terms(0, (0,), grads, d)
            rs_start(0)
        elif step + 1 < far:
            rs_step(0, step)
    for k in (1, 2):
        ag_finish(k)
    grads = hidden_grads(1, jnp.concatenate([xt[1], xt[2]], axis=1), pre_e[0], pre_e[1])
    for d in order[:3]:
        rs_terms(1, (1, 2), grads, d)
    for k in (1, 2):
        rs_start(k)
    rs_step(0, far - 1)
    for d in order[3:]:
        rs_terms(1, (1, 2), grads, d)
    for step in range(1, far):
        for k in (1, 2):
            rs_step(k, step)

    for h in range(2):
        back = rs_end(1 + h).astype(BF16)
        rows = dot(select[0], back[0:half], NT) + dot(select[1], back[half:], NT)
        returning[h * per : (h + 1) * per] = rows.reshape(per, rows8, half).astype(BF16)

        def send_back(i, carry):
            near = jnp.where(lax.div(e, per) == h, per // 2, 0)
            d = h * per + lax.rem(outward(e + near, i) + ne, per)

            @pl.when(d != e)
            def _():
                pltpu.make_async_remote_copy(
                    src_ref=returning.at[d],
                    dst_ref=returned.at[e],
                    send_sem=back_send,
                    recv_sem=back_recv,
                    device_id=(d, t),
                    device_id_type=MESH,
                ).start()

            @pl.when(d == e)
            def _():
                pltpu.make_async_copy(returning.at[d], returned.at[d], back_recv).start()

            return carry

        lax.fori_loop(0, per, send_back, 0)

    turned = small[...].T
    for k in range(2):
        for q in range(2):
            at = (2 * k + q) * tok
            picks[at : at + tok, :] = flag(
                iota((tok, ne * rows8), 1).astype(F32)
                == turned[0:tok, k : k + 1] + float(q * cap)
            )
    dense_sum[...] = rs_end(0).T

    for k in range(3):
        ref = xt.at[k, pl.ds(0, (nt - 1) * feat), :]
        pltpu.make_async_copy(ref, ref, ag_send.at[k]).wait()
        pltpu.make_async_copy(pair_out.at[k], pair_out.at[k], rs_send.at[k, 0]).wait()
        ref = pair_out.at[k, pl.ds(0, ny - 1)]
        pltpu.make_async_copy(ref, ref, rs_send.at[k, 1]).wait()
    ref = sent.at[pl.ds(0, ne - 1)]
    pltpu.make_async_copy(ref, ref, a2a_send).wait()
    ref = returning.at[pl.ds(0, ne - 1)]
    pltpu.make_async_copy(ref, ref, back_send).wait()

    pltpu.make_async_copy(returned, returned, back_recv).wait()
    rows = returned[...].astype(F32).reshape(ne * rows8, half).astype(BF16)
    picked = dot(picks[...], rows)
    dense = dense_sum[...]
    for q in range(2):
        total = dense[0:tok, q * half : (q + 1) * half]
        for k in range(2):
            at = (2 * k + q) * tok
            total = total + turned[0:tok, 2 + k : 3 + k] * picked[at : at + tok]
        result[:, q * half : (q + 1) * half] = total.astype(BF16)


def local(
    out_grad, dense_pre, dense_in, dense_out, routes, combine, expert_pre, expert_in, expert_out
):
    ne = lax.axis_size("expert")
    nt = lax.axis_size("tensor")
    ny = nt // 2
    far = ny // 2
    tok, feat = out_grad.shape
    units = dense_out.shape[0]
    slots = expert_pre.shape[1]
    cap = slots // ne
    lanes = slots // 2
    rows8 = 2 * cap
    half = feat // 2
    dim = nt * feat
    sizes = (ne, ny, tok, feat, units, cap, lanes)
    dma = pltpu.SemaphoreType.DMA
    scratch = [
        pltpu.VMEM((tok, feat), BF16),
        pltpu.VMEM((2, tok), jnp.int32),
        pltpu.VMEM((2, tok), F32),
        pltpu.VMEM((2, units, tok), BF16),
        pltpu.VMEM((2, units, slots), BF16),
        pltpu.VMEM((2, units, dim), BF16),
        pltpu.VMEM((2, 2, units, dim), BF16),
        pltpu.VMEM((2, 2, dim, units), BF16),
        pltpu.VMEM((8, 128), F32),
        pltpu.VMEM((4 * tok, ne * rows8), BF16),
        pltpu.VMEM((2, ne // 2 * rows8, lanes), BF16),
        pltpu.VMEM((ne, rows8, half), BF16),
        pltpu.VMEM((ne, rows8, half), BF16),
        pltpu.VMEM((ne, rows8, half), BF16),
        pltpu.VMEM((ne, rows8, half), BF16),
        pltpu.VMEM((3, dim, lanes), BF16),
        pltpu.VMEM((3, ny, feat, lanes), F32),
        pltpu.VMEM((3, ny, feat, lanes), BF16),
        pltpu.VMEM((3, ny, feat, lanes), BF16),
        pltpu.VMEM((3, 2, far, feat, lanes), BF16),
        pltpu.VMEM((3, 2, far, feat, lanes), BF16),
        pltpu.VMEM((lanes, feat), F32),
        dma((9,)),
        dma,
        dma((2,)),
        dma,
        dma,
        dma((3,)),
        dma((3, 2, far, 2)),
        dma((3, ny)),
        dma((3, 2)),
        dma((3, 2)),
        dma((3, 2, far, 2)),
        dma((3, ny)),
    ]
    any_spec = pl.BlockSpec(memory_space=pl.ANY)
    return pl.pallas_call(
        functools.partial(kernel, sizes),
        out_shape=pltpu.VMEM((tok, feat), BF16),
        in_specs=[any_spec] * 9,
        out_specs=pl.BlockSpec(memory_space=pltpu.VMEM),
        scratch_shapes=scratch,
        compiler_params=pltpu.CompilerParams(
            collective_id=0, has_side_effects=True, vmem_limit_bytes=56 * 1024 * 1024
        ),
    )(
        out_grad,
        routes.T,
        combine.T,
        dense_pre.transpose(1, 2, 0),
        expert_pre[0].transpose(1, 2, 0),
        dense_out,
        dense_in,
        expert_out[0],
        expert_in[0],
    )


def solution(mesh):
    return jax.shard_map(
        local,
        mesh=mesh,
        in_specs=(
            P("expert", "tensor"),
            P("expert", None, "tensor"),
            P(None, "tensor", None),
            P("tensor", None),
            P("expert", None),
            P("expert", None),
            P("expert", None, None, "tensor"),
            P("expert", None, "tensor", None),
            P("expert", "tensor", None),
        ),
        out_specs=P("expert", "tensor"),
        check_vma=False,
    )
```

```python
import functools

import jax
import jax.numpy as jnp
from jax import lax
from jax.experimental import pallas as pl
from jax.experimental.pallas import tpu as pltpu
from jax.sharding import PartitionSpec as P

BF16 = jnp.bfloat16
F32 = jnp.float32
MESH = pl.DeviceIdType.MESH
TN = (((0,), (0,)), ((), ()))
NT = (((1,), (1,)), ((), ()))


def dot(a, b, dims=(((1,), (0,)), ((), ()))):
    return lax.dot_general(a, b, dims, preferred_element_type=F32)


def iota(shape, dim):
    return lax.broadcasted_iota(jnp.int32, shape, dim)


def flag(mask):
    return jnp.where(mask, 1.0, 0.0).astype(BF16)


def kernel(
    sizes,
    og_hbm,
    rt_hbm,
    cb_hbm,
    pre_d_hbm,
    pre_e_hbm,
    out_d_hbm,
    in_d_hbm,
    out_e_hbm,
    in_e_hbm,
    result,
    og,
    rt,
    cb,
    pre_d,
    pre_e,
    w_out,
    w_in,
    w_in_t,
    small,
    picks,
    select,
    sent,
    arrived,
    returning,
    returned,
    xt,
    own_part,
    pair_out,
    pair_in,
    ring_out,
    ring_in,
    dense_sum,
    load_sem,
    a2a_send,
    a2a_recv,
    back_send,
    back_recv,
    ag_send,
    ag_ring,
    ag_pair,
    ag_cross,
    rs_send,
    rs_ring,
    rs_pair,
):
    ne, ny, tok, feat, units, cap, lanes = sizes
    nt = 2 * ny
    far = ny // 2
    half = feat // 2
    rows8 = 2 * cap
    per = ne // 2
    e = lax.axis_index("expert")
    t = lax.axis_index("tensor")
    y = lax.div(t, 2)
    c = lax.rem(t, 2)
    right = lax.rem(y + 1, ny) * 2 + c
    left = lax.rem(y + ny - 1, ny) * 2 + c
    sibling = y * 2 + (1 - c)

    def ring_pos(offset):
        return lax.rem(y + (offset + 2 * ny), ny)

    loads = [
        (rt_hbm, rt),
        (og_hbm, og),
        (cb_hbm, cb),
        (out_d_hbm, w_out.at[0]),
        (in_d_hbm, w_in.at[0]),
        (pre_d_hbm, pre_d),
        (out_e_hbm, w_out.at[1]),
        (in_e_hbm, w_in.at[1]),
        (pre_e_hbm, pre_e),
    ]
    loads = [pltpu.make_async_copy(a, b, load_sem.at[i]) for i, (a, b) in enumerate(loads)]
    for copy in loads:
        copy.start()

    barrier = pltpu.get_barrier_semaphore()
    across = [right + 1 - 2 * c, left + 1 - 2 * c]
    for peer in (right, left, sibling, across[0], across[1]):
        pl.semaphore_signal(barrier, inc=1, device_id=(e, peer), device_id_type=MESH)

    def outward(start, i):
        return start + jnp.where(lax.rem(i, 2) == 1, -lax.div(i + 1, 2), lax.div(i, 2))

    def greet(i, carry):
        d = lax.rem(outward(e + ne // 2, i) + ne, ne)
        pl.semaphore_signal(barrier, inc=1, device_id=(d, t), device_id_type=MESH)
        return carry

    lax.fori_loop(0, ne - 1, greet, 0)

    loads[0].wait()
    loads[1].wait()
    loads[2].wait()
    named = [iota((ne, tok), 0) == rt[k : k + 1, :] for k in range(2)]
    earlier = flag(iota((tok, tok), 0) < iota((tok, tok), 1))
    before = dot(flag(named[0] | named[1]), earlier)
    target = [
        rt[k : k + 1, :].astype(F32) * rows8
        + jnp.sum(jnp.where(named[k], before, 0.0), axis=0, keepdims=True)
        for k in range(2)
    ]
    grad = og[...]
    row = iota((ne * rows8, tok), 0).astype(F32)
    rows = None
    for q in range(2):
        match = (row == target[0] + float(q * cap)) | (row == target[1] + float(q * cap))
        term = dot(flag(match), grad[:, q * half : (q + 1) * half])
        rows = term if rows is None else rows + term
    sent[...] = rows.reshape(ne, rows8, half).astype(BF16)

    def block(k, o, part=None):
        if part is None:
            return xt.at[k, pl.ds(pl.multiple_of(o * feat, 16), feat), :]
        return xt.at[k, pl.ds(pl.multiple_of(o * feat + part * half, 16), half), :]

    block(0, t)[...] = dot(grad, flag(iota((tok, lanes), 0) == iota((tok, lanes), 1)), TN).astype(
        BF16
    )
    small[...] = jnp.zeros_like(small)
    for k in range(2):
        small[k : k + 1, 0:tok] = target[k]
        small[2 + k : 3 + k, 0:tok] = cb[k : k + 1, :]

    pl.semaphore_wait(barrier, ne - 1 + 5)

    def ag_ring_copy(k, way, step, part, source):
        ref = block(k, source * 2 + c, part)
        return pltpu.make_async_remote_copy(
            src_ref=ref,
            dst_ref=ref,
            send_sem=ag_send.at[k],
            recv_sem=ag_ring.at[k, way, step, part],
            device_id=(e, right if way == 0 else left),
            device_id_type=MESH,
        )

    def ag_pair_copy(k, index, source, core):
        ref = block(k, source * 2 + core)
        return pltpu.make_async_remote_copy(
            src_ref=ref,
            dst_ref=ref,
            send_sem=ag_send.at[k],
            recv_sem=ag_pair.at[k, index],
            device_id=(e, sibling),
            device_id_type=MESH,
        )

    def ag_cross_copy(k, way, source, core):
        ref = block(k, source * 2 + core, way)
        return pltpu.make_async_remote_copy(
            src_ref=ref,
            dst_ref=ref,
            send_sem=ag_send.at[k],
            recv_sem=ag_cross.at[k, way],
            device_id=(e, across[way]),
            device_id_type=MESH,
        )

    def ag_start(k):
        for i in range(2):
            for way in range(2):
                ag_ring_copy(k, way, 0, i if way == 0 else 1 - i, y).start()
        ag_pair_copy(k, 0, y, c).start()

    def ag_step(chunks, step):
        for k in chunks:
            for i in range(2 if step + 1 < far else 1):
                for way in range(2):
                    part = i if way == 0 else 1 - i
                    source = ring_pos(-1 - step if way == 0 else 1 + step)
                    ag_ring_copy(k, way, step, part, source).wait_recv()
                    if step + 2 < far or (step + 2 == far and i == 0):
                        ag_ring_copy(k, way, step + 1, part, source).start()
                    if step + 2 == far and i == 0:
                        ag_cross_copy(k, way, source, c).start()
        if step + 1 < far:
            for k in chunks:
                ag_pair_copy(k, 2 * step + 1, ring_pos(-1 - step), c).start()
                ag_pair_copy(k, 2 * step + 2, ring_pos(1 + step), c).start()

    def ag_finish(k):
        ag_pair_copy(k, 0, y, 1 - c).wait_recv()
        for step in range(far - 1):
            ag_pair_copy(k, 2 * step + 1, ring_pos(-1 - step), 1 - c).wait_recv()
            ag_pair_copy(k, 2 * step + 2, ring_pos(1 + step), 1 - c).wait_recv()
        for way in range(2):
            ag_cross_copy(k, way, ring_pos(far), 1 - c).wait_recv()

    def hidden_grads(w, x, pre_gate, pre_up):
        hidden = dot(w_out[w], x)
        gate = pre_gate.astype(F32)
        upper = pre_up.astype(F32)
        sig = jax.nn.sigmoid(gate)
        gate_grad = (hidden * upper * sig * (1.0 + gate * (1.0 - sig))).astype(BF16)
        up_grad = (hidden * gate * sig).astype(BF16)
        return gate_grad, up_grad

    order = [far]
    for d in range(far - 1, 0, -1):
        order += [d, -d]
    order += [0]

    def rs_pair_copy(k, pos):
        return pltpu.make_async_remote_copy(
            src_ref=pair_out.at[k, pos],
            dst_ref=pair_in.at[k, pos],
            send_sem=rs_send.at[k, 0],
            recv_sem=rs_pair.at[k, pos],
            device_id=(e, sibling),
            device_id_type=MESH,
        )

    def rs_terms(w, chunks, grads, d):
        pos = ring_pos(d)
        at = pl.ds(pl.multiple_of(pos * (2 * feat), 16), 2 * feat)
        both = dot(w_in_t[w, 0, at, :], grads[0]) + dot(w_in_t[w, 1, at, :], grads[1])
        other = lax.select(c == 0, both[feat:], both[:feat]).astype(BF16)
        own = lax.select(c == 0, both[:feat], both[feat:])
        for i, k in enumerate(chunks):
            pair_out[k, pos] = other[:, i * lanes : (i + 1) * lanes]
            rs_pair_copy(k, pos).start()
            own_part[k, pos] = own[:, i * lanes : (i + 1) * lanes]

    def rs_ring_copy(k, way, step, part):
        at = pl.ds(part * half, half)
        return pltpu.make_async_remote_copy(
            src_ref=ring_out.at[k, way, step, at, :],
            dst_ref=ring_in.at[k, way, step, at, :],
            send_sem=rs_send.at[k, 1],
            recv_sem=rs_ring.at[k, way, step, part],
            device_id=(e, right if way == 0 else left),
            device_id_type=MESH,
        )

    def rs_send_on(k, way, step, part, pos, add):
        at = pl.ds(part * half, half)
        total = own_part[k, pos, at, :] + pair_in[k, pos, at, :].astype(F32)
        if add:
            rs_ring_copy(k, way, step - 1, part).wait_recv()
            total = total + ring_in[k, way, step - 1, at, :].astype(F32)
        ring_out[k, way, step, at, :] = total.astype(BF16)
        rs_ring_copy(k, way, step, part).start()

    def rs_start(k):
        rs_pair_copy(k, ring_pos(far)).wait_recv()
        for way in range(2):
            rs_send_on(k, way, 0, way, ring_pos(far), False)

    def rs_step(k, step):
        spots = [ring_pos(far - step), ring_pos(step - far)]
        for way in range(2):
            rs_pair_copy(k, spots[way]).wait_recv()
        for i in range(2):
            for way in range(2):
                part = 1 - way if i == 0 else way
                rs_send_on(k, way, step, part, spots[way], step > 1 or part == way)

    def rs_end(k):
        rs_pair_copy(k, y).wait_recv()
        total = own_part[k, y] + pair_in[k, y].astype(F32)
        for way in range(2):
            for part in range(2):
                rs_ring_copy(k, way, far - 1, part).wait_recv()
            total = total + ring_in[k, way, far - 1].astype(F32)
        return total

    def a2a_copy(d):
        return pltpu.make_async_remote_copy(
            src_ref=sent.at[d],
            dst_ref=arrived.at[e],
            send_sem=a2a_send,
            recv_sem=a2a_recv.at[lax.div(e, per)],
            device_id=(d, t),
            device_id_type=MESH,
        )

    def a2a_start(i, carry):
        a2a_copy(lax.rem(outward(e + ne // 2, i) + ne, ne)).start()
        return carry

    def a2a_wait(h):
        ref = arrived.at[pl.ds(h * per, per)]
        pltpu.make_async_copy(ref, ref, a2a_recv.at[h]).wait()

    def fill_select(q):
        n = iota((per * rows8, lanes), 1)
        r = iota((per * rows8, lanes), 0)
        select[q] = flag(r == lax.div(n, cap) * rows8 + q * cap + lax.rem(n, cap))

    def take_rows(h):
        rows = arrived[h * per : (h + 1) * per].astype(F32).reshape(per * rows8, half).astype(BF16)
        for q in range(2):
            block(1 + h, t, q)[...] = dot(rows, select[q], TN).astype(BF16)

    piece = min(256, nt * feat)
    pieces = nt * feat // piece

    def turn(w, first, last):
        eye = flag(iota((piece, piece), 0) == iota((piece, piece), 1))

        def one(j, carry):
            at = pl.ds(pl.multiple_of(j * piece, piece), piece)
            for m in range(2):
                w_in_t[w, m, at, :] = dot(eye, w_in[w, m, :, at], NT).astype(BF16)
            return carry

        lax.fori_loop(first, last, one, 0)

    ag_start(0)
    pltpu.make_async_copy(sent.at[e], arrived.at[e], a2a_recv.at[lax.div(e, per)]).start()
    lax.fori_loop(0, ne - 1, a2a_start, 0)
    loads[4].wait()
    for q in range(2):
        fill_select(q)
    turn(0, 0, pieces // 2)
    ag_step((0,), 0)
    turn(0, pieces // 2, pieces)
    ag_step((0,), 1)
    loads[7].wait()
    turn(1, 0, pieces // 2)
    for step in range(2, far - 1):
        ag_step((0,), step)
    turn(1, pieces // 2, pieces)
    for i in (3, 5, 6, 8):
        loads[i].wait()
    for h in range(2):
        a2a_wait(h)
        take_rows(h)
        ag_start(1 + h)
    for step in range(max(2, far - 1), far):
        ag_step((0,), step)
    ag_finish(0)
    fill = jnp.zeros((units, lanes - tok), BF16)
    pre = [jnp.concatenate([pre_d[m], fill], axis=1) if lanes > tok else pre_d[m] for m in range(2)]
    grads = hidden_grads(0, xt[0], pre[0], pre[1])
    for d in order[:2]:
        rs_terms(0, (0,), grads, d)
    for step in range(far):
        ag_step((1, 2), step)
        if step == 0:
            for d in order[2:]:
                rs_terms(0, (0,), grads, d)
            rs_start(0)
        elif step == 1 and far > 2:
            rs_step(0, step)
    for k in (1, 2):
        ag_finish(k)
    grads = hidden_grads(1, jnp.concatenate([xt[1], xt[2]], axis=1), pre_e[0], pre_e[1])
    for d in order[:3]:
        rs_terms(1, (1, 2), grads, d)
    for k in (1, 2):
        rs_start(k)
    for d in order[3:]:
        rs_terms(1, (1, 2), grads, d)
    for step in range(1, far):
        for k in (1, 2):
            rs_step(k, step)

    for h in range(2):
        back = rs_end(1 + h).astype(BF16)
        rows = dot(select[0], back[0:half], NT) + dot(select[1], back[half:], NT)
        returning[h * per : (h + 1) * per] = rows.reshape(per, rows8, half).astype(BF16)

        def send_back(i, carry):
            near = jnp.where(lax.div(e, per) == h, per // 2, 0)
            d = h * per + lax.rem(outward(e + near, i) + ne, per)

            @pl.when(d != e)
            def _():
                pltpu.make_async_remote_copy(
                    src_ref=returning.at[d],
                    dst_ref=returned.at[e],
                    send_sem=back_send,
                    recv_sem=back_recv,
                    device_id=(d, t),
                    device_id_type=MESH,
                ).start()

            @pl.when(d == e)
            def _():
                pltpu.make_async_copy(returning.at[d], returned.at[d], back_recv).start()

            return carry

        lax.fori_loop(0, per, send_back, 0)

    for step in range(2 if far > 2 else 1, far - 1):
        rs_step(0, step)
    turned = small[...].T
    for k in range(2):
        for q in range(2):
            at = (2 * k + q) * tok
            picks[at : at + tok, :] = flag(
                iota((tok, ne * rows8), 1).astype(F32)
                == turned[0:tok, k : k + 1] + float(q * cap)
            )
    rs_step(0, far - 1)
    dense_sum[...] = rs_end(0).T

    for k in range(3):
        ref = xt.at[k, pl.ds(0, (nt - 1) * feat), :]
        pltpu.make_async_copy(ref, ref, ag_send.at[k]).wait()
        pltpu.make_async_copy(pair_out.at[k], pair_out.at[k], rs_send.at[k, 0]).wait()
        ref = pair_out.at[k, pl.ds(0, ny - 1)]
        pltpu.make_async_copy(ref, ref, rs_send.at[k, 1]).wait()
    ref = sent.at[pl.ds(0, ne - 1)]
    pltpu.make_async_copy(ref, ref, a2a_send).wait()
    ref = returning.at[pl.ds(0, ne - 1)]
    pltpu.make_async_copy(ref, ref, back_send).wait()

    pltpu.make_async_copy(returned, returned, back_recv).wait()
    rows = returned[...].astype(F32).reshape(ne * rows8, half).astype(BF16)
    picked = dot(picks[...], rows)
    dense = dense_sum[...]
    for q in range(2):
        total = dense[0:tok, q * half : (q + 1) * half]
        for k in range(2):
            at = (2 * k + q) * tok
            total = total + turned[0:tok, 2 + k : 3 + k] * picked[at : at + tok]
        result[:, q * half : (q + 1) * half] = total.astype(BF16)


def local(
    out_grad, dense_pre, dense_in, dense_out, routes, combine, expert_pre, expert_in, expert_out
):
    ne = lax.axis_size("expert")
    nt = lax.axis_size("tensor")
    ny = nt // 2
    far = ny // 2
    tok, feat = out_grad.shape
    units = dense_out.shape[0]
    slots = expert_pre.shape[1]
    cap = slots // ne
    lanes = slots // 2
    rows8 = 2 * cap
    half = feat // 2
    dim = nt * feat
    sizes = (ne, ny, tok, feat, units, cap, lanes)
    dma = pltpu.SemaphoreType.DMA
    scratch = [
        pltpu.VMEM((tok, feat), BF16),
        pltpu.VMEM((2, tok), jnp.int32),
        pltpu.VMEM((2, tok), F32),
        pltpu.VMEM((2, units, tok), BF16),
        pltpu.VMEM((2, units, slots), BF16),
        pltpu.VMEM((2, units, dim), BF16),
        pltpu.VMEM((2, 2, units, dim), BF16),
        pltpu.VMEM((2, 2, dim, units), BF16),
        pltpu.VMEM((8, 128), F32),
        pltpu.VMEM((4 * tok, ne * rows8), BF16),
        pltpu.VMEM((2, ne // 2 * rows8, lanes), BF16),
        pltpu.VMEM((ne, rows8, half), BF16),
        pltpu.VMEM((ne, rows8, half), BF16),
        pltpu.VMEM((ne, rows8, half), BF16),
        pltpu.VMEM((ne, rows8, half), BF16),
        pltpu.VMEM((3, dim, lanes), BF16),
        pltpu.VMEM((3, ny, feat, lanes), F32),
        pltpu.VMEM((3, ny, feat, lanes), BF16),
        pltpu.VMEM((3, ny, feat, lanes), BF16),
        pltpu.VMEM((3, 2, far, feat, lanes), BF16),
        pltpu.VMEM((3, 2, far, feat, lanes), BF16),
        pltpu.VMEM((lanes, feat), F32),
        dma((9,)),
        dma,
        dma((2,)),
        dma,
        dma,
        dma((3,)),
        dma((3, 2, far, 2)),
        dma((3, ny)),
        dma((3, 2)),
        dma((3, 2)),
        dma((3, 2, far, 2)),
        dma((3, ny)),
    ]
    any_spec = pl.BlockSpec(memory_space=pl.ANY)
    return pl.pallas_call(
        functools.partial(kernel, sizes),
        out_shape=pltpu.VMEM((tok, feat), BF16),
        in_specs=[any_spec] * 9,
        out_specs=pl.BlockSpec(memory_space=pltpu.VMEM),
        scratch_shapes=scratch,
        compiler_params=pltpu.CompilerParams(
            collective_id=0, has_side_effects=True, vmem_limit_bytes=56 * 1024 * 1024
        ),
    )(
        out_grad,
        routes.T,
        combine.T,
        dense_pre.transpose(1, 2, 0),
        expert_pre[0].transpose(1, 2, 0),
        dense_out,
        dense_in,
        expert_out[0],
        expert_in[0],
    )


def solution(mesh):
    return jax.shard_map(
        local,
        mesh=mesh,
        in_specs=(
            P("expert", "tensor"),
            P("expert", None, "tensor"),
            P(None, "tensor", None),
            P("tensor", None),
            P("expert", None),
            P("expert", None),
            P("expert", None, None, "tensor"),
            P("expert", None, "tensor", None),
            P("expert", "tensor", None),
        ),
        out_specs=P("expert", "tensor"),
        check_vma=False,
    )
```
